32 devices in a mesh: mem: 4 (over z), pipe: 4 (over y, x), dp: 2 (over core).
Axes of the slice: x: 2, y: 2, z: 4, core: 2. Of those that a mesh axis runs over, the one named last changes fastest.
Arguments:
- values: bfloat16 [4096, 4096], P(('dp', 'mem'), 'pipe'), parts along dimension 0, may hold values from -6 to 6
- cotangent: bfloat16 [1024, 4096], P(('dp', 'mem'), 'pipe'), parts along dimension 0, may hold values from -6 to 6
- scores: float32 [1024, 4, 32], P(('dp', 'mem')), parts along dimension 0, may hold values from -8 to 410, as said below
- row_lists: int32 [8, 4, 128], P(('dp', 'mem')), parts along dimension 0, may hold values from -1 to 511, as said below
- sel_slot: int32 [1024, 4, 32], P(('dp', 'mem')), parts along dimension 0, may hold values from 0 to 511, as said below
Outputs:
- mem_out: bfloat16 [1024, 4096], P(('dp', 'mem'), 'pipe'), parts along dimension 0
- grad_values: bfloat16 [4096, 4096], P(('dp', 'mem'), 'pipe'), parts along dimension 0
- grad_scores: float32 [1024, 4, 32], P(('dp', 'mem')), parts along dimension 0
The draws below stay inside these ranges and needn't reach their ends.
There are 2 independent parts, one for each index of `dp`. The reference program is written for one: setup_inputs(seed, part) draws one part's arguments, and reference() takes and returns one part's arrays. A program takes and returns all parts, laid end to end along the dimension named above; each array names one. Nothing has to cross between parts.
Inputs may be any that keep to these rules, and one draw needn't show every extreme that they name: `row_lists`: each entry is a row of the owner's shard, or -1 for an empty slot; the rows of one block are distinct and its empty slots come last; in every draw some owner receives full blocks of 128 rows from every device. `sel_slot`: each entry names a slot of the request blocks of the token's own mem index, and that slot holds a row; the 32 entries of one token and head are distinct. `scores`: scores are finite.
All inputs are finite; a program needn't handle non-finite values.
Results may differ from the reference program's by a relative error of at most 0.013.
Values may be sent and summed in bfloat16 or wider, within the bound.
A program may use at most 128 MiB of HBM per device.

```python
import jax
import jax.numpy as jnp
from jax import lax

D = 4096
HEADS = 4
TOPK = 32
CAP = 128
TOK_DEV = 128
ROWS_DEV = 512
OWNERS = 4
TOKENS = 512
ROWS = 2048


def block_counts(key):
    base = jax.random.fold_in(key, 7)
    hot = max(1, OWNERS // 8)
    order = jax.random.permutation(jax.random.fold_in(base, 1), OWNERS)
    owner_ids = jnp.arange(OWNERS, dtype=jnp.int32)
    is_hot = jnp.any(owner_ids[:, None] == order[None, :hot], axis=1)
    counts = jax.random.randint(jax.random.fold_in(base, 2), (OWNERS, OWNERS), max(1, CAP // 8), CAP // 2 + 1)
    return jnp.where(is_hot[None, :], CAP, counts).astype(jnp.int32)


def draw_row_lists(key, part):
    counts = block_counts(key)
    ranks = jax.random.randint(jax.random.fold_in(key, 3), (OWNERS, OWNERS, ROWS_DEV), 0, 4096)
    keyed = ranks * ROWS_DEV + jnp.arange(ROWS_DEV, dtype=jnp.int32)
    order = jnp.argsort(keyed, axis=-1)[..., :CAP].astype(jnp.int32)
    valid = jnp.arange(CAP, dtype=jnp.int32)[None, None, :] < counts[..., None]
    return jnp.where(valid, order, -1).astype(jnp.int32)


def draw_sel_slot(key, part):
    counts = block_counts(key)
    slot_ids = jnp.arange(OWNERS * CAP, dtype=jnp.int32)
    valid = (slot_ids % CAP)[None, :] < jnp.repeat(counts, CAP, axis=1)
    pick_key = jax.random.fold_in(key, 5)

    def one_sender(sender):
        ranks = jax.random.randint(jax.random.fold_in(pick_key, sender), (TOK_DEV * HEADS, OWNERS * CAP), 1, 4096)
        keyed = ranks * (OWNERS * CAP) + slot_ids[None, :]
        keyed = jnp.where(valid[sender][None, :], keyed, -1)
        return lax.top_k(keyed, TOPK)[1].astype(jnp.int32)
    picks = lax.map(one_sender, jnp.arange(OWNERS, dtype=jnp.int32))
    return picks.reshape(TOKENS, HEADS, TOPK)


def draw_scores(key, part):
    shape = (TOKENS, HEADS, TOPK)
    drawn = jax.random.normal(jax.random.fold_in(key, 1), shape, jnp.float32)
    return jnp.clip(2.0 * drawn, -8.0, 8.0).astype(jnp.float32)


def steps_of(own_key, shape, split, low, high):
    factor_of, own = 1.0, jax.random.fold_in(own_key, 6)
    for dim, shards_of in split:
        heights = jnp.exp(jax.random.uniform(jax.random.fold_in(own, dim), (shards_of,), jnp.float32, low / len(split), high / len(split)))
        factor_of = factor_of * jnp.repeat(heights, shape[dim] // shards_of).reshape([-1 if axis == dim else 1 for axis in range(len(shape))])
    return factor_of


def scatter_about(stream_key, extent, deviation, limit, cuts=(), held_as=jnp.bfloat16):
    values = jax.random.normal(stream_key, extent, jnp.float32) * deviation
    if len(cuts) > 0:
        values = steps_of(stream_key, extent, cuts, -0.22, 0.18) * values
    return jnp.clip(values, min=-limit, max=limit).astype(held_as)


def setup_inputs(seed: int = 0, part: int = 0) -> dict:
    key_of = jax.random.split(jax.random.key(seed), 6)
    own_keys = jax.random.split(jax.random.fold_in(key_of[5], part), 6)
    values = scatter_about(own_keys[0], (ROWS, D), 1.0, 6.0, ((0, 4), (1, 4)))
    cotangent = scatter_about(own_keys[1], (TOKENS, D), 1.0, 6.0, ((0, 4), (1, 4)))
    scores = draw_scores(jax.random.fold_in(jax.random.fold_in(key_of[5], part), 71), part)
    row_lists = draw_row_lists(jax.random.fold_in(jax.random.fold_in(key_of[5], part), 71), part)
    sel_slot = draw_sel_slot(jax.random.fold_in(jax.random.fold_in(key_of[5], part), 71), part)
    return dict(values=values, cotangent=cotangent, scores=scores, row_lists=row_lists, sel_slot=sel_slot)


def reference(values, cotangent, scores, row_lists, sel_slot):
    slot_count = OWNERS * CAP
    weights = jax.nn.softmax(scores.astype(jnp.float32), axis=-1)
    owner_base = jnp.arange(OWNERS, dtype=jnp.int32)[:, None] * ROWS_DEV

    def per_sender(carry, sender):
        lists = lax.dynamic_index_in_dim(row_lists, sender, 0, keepdims=False)
        global_rows = (owner_base + jnp.maximum(lists, 0)).reshape(-1).astype(jnp.int32)
        gathered = jnp.take(values, global_rows, axis=0)
        start = (sender * TOK_DEV).astype(jnp.int32)
        w_here = lax.dynamic_slice_in_dim(weights, start, TOK_DEV, 0)
        sel_here = lax.dynamic_slice_in_dim(sel_slot, start, TOK_DEV, 0)
        cot_here = lax.dynamic_slice_in_dim(cotangent, start, TOK_DEV, 0)
        chosen = sel_here.reshape(TOK_DEV, -1)
        flat_index = (jnp.arange(TOK_DEV, dtype=jnp.int32)[:, None] * slot_count + chosen).reshape(-1)
        combined = jnp.zeros((TOK_DEV * slot_count,), jnp.float32).at[flat_index].add(w_here.reshape(-1))
        combined = combined.reshape(TOK_DEV, slot_count).astype(jnp.bfloat16)
        out_here = jnp.dot(combined, gathered, preferred_element_type=jnp.float32).astype(jnp.bfloat16)
        products = jnp.dot(cot_here, gathered.T, preferred_element_type=jnp.float32)
        dots = jnp.take_along_axis(products, chosen, axis=1).reshape(w_here.shape)
        dscore = w_here * (dots - jnp.sum(w_here * dots, axis=-1, keepdims=True))
        contrib = jnp.dot(combined.T, cot_here, preferred_element_type=jnp.float32)
        target = jnp.where(lists.reshape(-1) >= 0, global_rows, ROWS).astype(jnp.int32)
        carry = carry.at[target].add(contrib)
        return carry, (out_here, dscore)

    start_grad = jnp.zeros((ROWS + 1, D), jnp.float32)
    grad_all, (outs, dscores) = lax.scan(per_sender, start_grad, jnp.arange(OWNERS, dtype=jnp.int32))
    mem_out = outs.reshape(TOKENS, D)
    grad_values = grad_all[:ROWS].astype(jnp.bfloat16)
    grad_scores = dscores.reshape(TOKENS, HEADS, TOPK)
    return mem_out, grad_values, grad_scores
```

```python
import functools

import jax
import jax.numpy as jnp
from jax import lax
from jax.experimental import pallas as pl
from jax.experimental.pallas import tpu as pltpu
from jax.sharding import PartitionSpec as P


def shards_collective(values, cotangent, scores, row_lists, sel_slot):
    owners = lax.axis_size("mem")
    tokens_here = cotangent.shape[0]
    cap_slots = row_lists.shape[2]
    slot_count = owners * cap_slots
    width = values.shape[1]
    table_rows = values.shape[0]
    highest = lax.Precision.HIGHEST
    weights = jax.nn.softmax(scores, axis=-1)
    chosen = sel_slot.reshape(tokens_here, -1)
    owner_of = chosen // cap_slots
    place_of = chosen % cap_slots
    owner_hot = (owner_of[..., None] == jnp.arange(owners, dtype=jnp.int32)[None, None, :]).astype(
        jnp.float32
    )
    place_hot = (
        place_of[..., None] == jnp.arange(cap_slots, dtype=jnp.int32)[None, None, :]
    ).astype(jnp.float32)
    weighted_owner = owner_hot * weights.reshape(tokens_here, -1)[..., None]
    combined = jnp.einsum(
        "tpo,tpc->toc",
        weighted_owner,
        place_hot,
        precision=highest,
        preferred_element_type=jnp.float32,
    )
    combined = combined.reshape(tokens_here, slot_count).astype(jnp.bfloat16)
    asked = lax.all_to_all(row_lists[0], "mem", split_axis=0, concat_axis=0, tiled=True)
    present = asked >= 0
    looked = jnp.take(values, jnp.maximum(asked, 0), axis=0)
    looked = jnp.where(present[..., None], looked, jnp.zeros_like(looked))
    replied = lax.all_to_all(looked, "mem", split_axis=0, concat_axis=0, tiled=True)
    gathered_rows = replied.reshape(slot_count, width)
    mem_out = jnp.dot(combined, gathered_rows, preferred_element_type=jnp.float32).astype(
        jnp.bfloat16
    )
    products = lax.dot_general(
        cotangent, gathered_rows, (((1,), (1,)), ((), ())), preferred_element_type=jnp.float32
    )
    products = products.reshape(tokens_here, owners, cap_slots)
    picked = jnp.einsum(
        "tpc,toc->tpo", place_hot, products, precision=highest, preferred_element_type=jnp.float32
    )
    partial_dots = jnp.sum(picked * owner_hot, axis=-1).reshape(weights.shape)
    full_dots = lax.psum(partial_dots.astype(jnp.bfloat16), "pipe").astype(jnp.float32)
    grad_scores = weights * (full_dots - jnp.sum(weights * full_dots, axis=-1, keepdims=True))
    sums_here = lax.dot_general(
        combined, cotangent, (((0,), (0,)), ((), ())), preferred_element_type=jnp.float32
    )
    received = lax.all_to_all(
        sums_here.reshape(owners, cap_slots, width).astype(jnp.bfloat16),
        "mem",
        split_axis=0,
        concat_axis=0,
        tiled=True,
    ).astype(jnp.float32)
    received = received.reshape(-1, width)
    upper_part = received.astype(jnp.bfloat16)
    lower_part = (received - upper_part.astype(jnp.float32)).astype(jnp.bfloat16)
    row_hot = (
        asked.reshape(-1)[:, None] == jnp.arange(table_rows, dtype=jnp.int32)[None, :]
    ).astype(jnp.bfloat16)
    contract = (((0,), (0,)), ((), ()))
    grad_full = lax.dot_general(row_hot, upper_part, contract, preferred_element_type=jnp.float32)
    grad_full = grad_full + lax.dot_general(
        row_hot, lower_part, contract, preferred_element_type=jnp.float32
    )
    grad_values = grad_full.astype(jnp.bfloat16)
    return (mem_out, grad_values, grad_scores)


MESH = pl.DeviceIdType.MESH
CHUNKS = 4
F32 = jnp.float32
BF16 = jnp.bfloat16


def kernel(
    n,
    pipes,
    heads,
    topk,
    values_ref,
    cot_ref,
    scores_ref,
    rows_ref,
    sel_ref,
    mem_ref,
    grad_ref,
    dscore_ref,
    cot_all,
    weights,
    comb_own,
    comb_in,
    rows_in,
    hot,
    spread,
    part,
    from_left,
    from_right,
    prod_out,
    prod_in,
    dots_in,
    ag_send,
    ag_recv,
    cb_send,
    cb_recv,
    rl_send,
    rl_recv,
    rs_send,
    rs_recv,
    pr_send,
    pr_recv,
    dt_send,
    dt_recv,
):
    me = lax.axis_index("mem")
    my_pipe = lax.axis_index("pipe")
    tokens, width = cot_ref.shape
    table_rows = values_ref.shape[0]
    cap = rows_ref.shape[2]
    step = tokens // CHUNKS
    picks = heads * topk

    def peer(d):
        return lax.rem(me + d, n)

    def pipe_peer(d):
        return lax.rem(my_pipe + d, pipes)

    barrier = pltpu.get_barrier_semaphore()
    for d in range(1, n):
        pl.semaphore_signal(barrier, inc=1, device_id={"mem": peer(d)}, device_id_type=MESH)
    for d in range(1, pipes):
        pl.semaphore_signal(
            barrier, inc=1, device_id={"pipe": pipe_peer(d)}, device_id_type=MESH
        )
    pl.semaphore_wait(barrier, n - 1 + pipes - 1)

    def rows_of(c):
        return pl.ds(c * step, step)

    def gather_copy(side, source, c, own=False):
        to = me + 1 if side == 0 else me - 1
        src = cot_ref.at[rows_of(c)] if own else cot_all.at[source, rows_of(c)]
        return pltpu.make_async_remote_copy(
            src_ref=src,
            dst_ref=cot_all.at[source, rows_of(c)],
            send_sem=ag_send.at[side, source, c],
            recv_sem=ag_recv.at[source, c],
            device_id={"mem": to},
            device_id_type=MESH,
        )

    def sum_copy(side, dest, c):
        to = me + 1 if side == 0 else me - 1
        buf = from_left if side == 0 else from_right
        return pltpu.make_async_remote_copy(
            src_ref=buf.at[dest, rows_of(c)],
            dst_ref=buf.at[dest, rows_of(c)],
            send_sem=rs_send.at[side, dest, c],
            recv_sem=rs_recv.at[side, dest, c],
            device_id={"mem": to},
            device_id_type=MESH,
        )

    def list_copy(to):
        return pltpu.make_async_remote_copy(
            src_ref=rows_ref.at[to],
            dst_ref=rows_in.at[me],
            send_sem=rl_send.at[to],
            recv_sem=rl_recv.at[me],
            device_id={"mem": to},
            device_id_type=MESH,
        )

    def list_arrival(source):
        return pltpu.make_async_remote_copy(
            src_ref=rows_in.at[source],
            dst_ref=rows_in.at[source],
            send_sem=rl_send.at[source],
            recv_sem=rl_recv.at[source],
            device_id={"mem": source},
            device_id_type=MESH,
        )

    def comb_copy(to):
        return pltpu.make_async_remote_copy(
            src_ref=comb_own.at[to],
            dst_ref=comb_in.at[me],
            send_sem=cb_send.at[to],
            recv_sem=cb_recv.at[me],
            device_id={"mem": to},
            device_id_type=MESH,
        )

    def comb_arrival(source):
        return pltpu.make_async_remote_copy(
            src_ref=comb_in.at[source],
            dst_ref=comb_in.at[source],
            send_sem=cb_send.at[source],
            recv_sem=cb_recv.at[source],
            device_id={"mem": source},
            device_id_type=MESH,
        )

    def prod_copy(to):
        return pltpu.make_async_remote_copy(
            src_ref=prod_out.at[to],
            dst_ref=prod_in.at[me],
            send_sem=pr_send.at[to],
            recv_sem=pr_recv.at[me],
            device_id={"mem": to},
            device_id_type=MESH,
        )

    def prod_arrival(source):
        return pltpu.make_async_remote_copy(
            src_ref=prod_in.at[source],
            dst_ref=prod_in.at[source],
            send_sem=pr_send.at[source],
            recv_sem=pr_recv.at[source],
            device_id={"mem": source},
            device_id_type=MESH,
        )

    def dots_copy(to):
        return pltpu.make_async_remote_copy(
            src_ref=dots_in.at[my_pipe],
            dst_ref=dots_in.at[my_pipe],
            send_sem=dt_send.at[to],
            recv_sem=dt_recv.at[my_pipe],
            device_id={"pipe": to},
            device_id_type=MESH,
        )

    def dots_arrival(source):
        return pltpu.make_async_remote_copy(
            src_ref=dots_in.at[source],
            dst_ref=dots_in.at[source],
            send_sem=dt_send.at[source],
            recv_sem=dt_recv.at[source],
            device_id={"pipe": source},
            device_id_type=MESH,
        )

    for d in range(1, n):
        list_copy(peer(d)).start()
    for c in range(CHUNKS):

        @pl.when(me < n - 1)
        def _():
            gather_copy(0, me, c, own=True).start()

        @pl.when(me > 0)
        def _():
            gather_copy(1, me, c, own=True).start()

    rows_in[me] = rows_ref[me]
    cot_all[me] = cot_ref[...]

    scores = scores_ref[...]
    raised = jnp.exp(scores - jnp.max(scores, axis=1, keepdims=True))
    share = raised / jnp.sum(raised, axis=1, keepdims=True)
    weights[...] = share.reshape(picks, tokens)

    place = lax.broadcasted_iota(jnp.int32, (cap, tokens), 0)

    @pl.loop(0, n)
    def _(owner):
        first = owner * cap
        total = jnp.zeros((cap, tokens), F32)
        for h in range(heads):
            held = jnp.zeros((cap, tokens), F32)
            for k in range(topk):
                p = h * topk + k
                here = sel_ref[p : p + 1, :] - first
                held = jnp.where(place == here, weights[p : p + 1, :], held)
            total = total + held
        comb_own[owner] = total.astype(BF16)

    for d in range(1, n):
        comb_copy(peer(d)).start()
    comb_in[me] = comb_own[me]

    def relay(d):
        for c in range(CHUNKS):

            @pl.when(me - d >= 0)
            def _():
                gather_copy(0, me - d, c).wait_recv()

            @pl.when((me - d >= 0) & (me < n - 1))
            def _():
                gather_copy(0, me - d, c).start()

            @pl.when(me + d < n)
            def _():
                gather_copy(1, me + d, c).wait_recv()

            @pl.when((me + d < n) & (me > 0))
            def _():
                gather_copy(1, me + d, c).start()

    relay(1)

    row_ids = lax.broadcasted_iota(jnp.int32, (table_rows, cap), 0)
    for d in range(1, n):
        list_arrival(peer(d)).wait_recv()
        comb_arrival(peer(d)).wait_recv()
    for s in range(n):
        hot[s] = jnp.where(rows_in[s] == row_ids, 1.0, 0.0).astype(BF16)
        spread[:, s * tokens : (s + 1) * tokens] = jnp.dot(
            hot[s], comb_in[s], preferred_element_type=F32
        ).astype(BF16)
    part[...] = lax.dot_general(
        spread[...], values_ref[...], (((0,), (0,)), ((), ())), preferred_element_type=F32
    ).reshape(n, tokens, width)

    def pass_on(t):
        right_dest = n - 1 - t + me
        left_dest = t - (n - 1 - me)
        for c in range(CHUNKS):
            at = rows_of(c)

            @pl.when((t >= me) & (me == 0))
            def _():
                from_left[right_dest, at] = part[right_dest, at].astype(BF16)

            @pl.when((t >= me) & (me > 0))
            def _():
                sum_copy(0, right_dest, c).wait_recv()
                got = from_left[right_dest, at].astype(F32)
                from_left[right_dest, at] = (got + part[right_dest, at]).astype(BF16)

            @pl.when(t >= me)
            def _():
                sum_copy(0, right_dest, c).start()

            @pl.when((left_dest >= 0) & (me == n - 1))
            def _():
                from_right[left_dest, at] = part[left_dest, at].astype(BF16)

            @pl.when((left_dest >= 0) & (me < n - 1))
            def _():
                sum_copy(1, left_dest, c).wait_recv()
                got = from_right[left_dest, at].astype(F32)
                from_right[left_dest, at] = (got + part[left_dest, at]).astype(BF16)

            @pl.when(left_dest >= 0)
            def _():
                sum_copy(1, left_dest, c).start()

    def products(source):
        full = lax.dot_general(
            cot_all[source],
            values_ref[...],
            (((1,), (1,)), ((), ())),
            preferred_element_type=F32,
        ).astype(BF16)
        prod_out[source] = jnp.dot(full, hot[source], preferred_element_type=F32).astype(BF16)

    def products_at(d):
        @pl.when(me - d >= 0)
        def _():
            products(me - d)
            prod_copy(me - d).start()

        @pl.when(me + d < n)
        def _():
            products(me + d)
            prod_copy(me + d).start()

    pass_on(0)
    products(me)
    prod_in[me] = prod_out[me]
    products_at(1)
    for d in range(2, n):
        relay(d)
        pass_on(d - 1)
        products_at(d)

    for column in range(0, width, 256):
        grad_ref[:, column : column + 256] = jnp.dot(
            spread[...],
            cot_all[:, :, column : column + 256].reshape(n * tokens, 256),
            preferred_element_type=F32,
        ).astype(BF16)

    for d in range(1, n):
        prod_arrival(peer(d)).wait_recv()
    chosen = sel_ref[...].T
    place_of = lax.rem(chosen, cap)
    owner_of = lax.div(chosen, cap)
    dots = jnp.zeros((tokens, picks), F32)
    for o in range(n):
        found = jnp.take_along_axis(
            prod_in[o].astype(F32), place_of, axis=1, mode="promise_in_bounds"
        )
        dots = jnp.where(owner_of == o, found, dots)
    dots_in[my_pipe] = dots.T.astype(BF16)
    for d in range(1, pipes):
        dots_copy(pipe_peer(d)).start()

    for c in range(CHUNKS):
        at = rows_of(c)
        part_here = part[me, at]

        mem_ref[at] = part_here.astype(BF16)

        @pl.when((me > 0) & (me < n - 1))
        def _():
            sum_copy(0, me, c).wait_recv()
            sum_copy(1, me, c).wait_recv()
            both = from_left[me, at].astype(F32) + from_right[me, at].astype(F32)
            mem_ref[at] = (part[me, at] + both).astype(BF16)

        @pl.when(me == 0)
        def _():
            sum_copy(1, me, c).wait_recv()
            mem_ref[at] = (part[me, at] + from_right[me, at].astype(F32)).astype(BF16)

        @pl.when(me == n - 1)
        def _():
            sum_copy(0, me, c).wait_recv()
            mem_ref[at] = (part[me, at] + from_left[me, at].astype(F32)).astype(BF16)

    for d in range(1, pipes):
        dots_arrival(pipe_peer(d)).wait_recv()
    full_dots = dots_in[0].astype(F32)
    for q in range(1, pipes):
        full_dots = full_dots + dots_in[q].astype(F32)
    full_dots = full_dots.reshape(heads, topk, tokens)
    w = weights[...].reshape(heads, topk, tokens)
    dscore_ref[...] = w * (full_dots - jnp.sum(w * full_dots, axis=1, keepdims=True))

    for d in range(1, n):
        list_copy(peer(d)).wait_send()
        comb_copy(peer(d)).wait_send()
        prod_copy(peer(d)).wait_send()
    for d in range(1, pipes):
        dots_copy(pipe_peer(d)).wait_send()
    for c in range(CHUNKS):
        for d in range(n - 1):

            @pl.when((me - d >= 0) & (me < n - 1))
            def _():
                gather_copy(0, me - d, c, own=d == 0).wait_send()

            @pl.when((me + d < n) & (me > 0))
            def _():
                gather_copy(1, me + d, c, own=d == 0).wait_send()

        for t in range(n - 1):
            right_dest = n - 1 - t + me
            left_dest = t - (n - 1 - me)

            @pl.when(t >= me)
            def _():
                sum_copy(0, right_dest, c).wait_send()

            @pl.when(left_dest >= 0)
            def _():
                sum_copy(1, left_dest, c).wait_send()


def shards_kernel(values, cotangent, scores, row_lists, sel_slot):
    n, pipes = lax.axis_size("mem"), lax.axis_size("pipe")
    tokens, width = cotangent.shape
    heads, topk = scores.shape[1:]
    table_rows, cap = values.shape[0], row_lists.shape[2]
    picks = heads * topk
    dma = pltpu.SemaphoreType.DMA
    mem_out, grad_values, dscore = pl.pallas_call(
        functools.partial(kernel, n, pipes, heads, topk),
        out_shape=(
            jax.ShapeDtypeStruct((tokens, width), BF16),
            jax.ShapeDtypeStruct((table_rows, width), BF16),
            jax.ShapeDtypeStruct((heads, topk, tokens), F32),
        ),
        in_specs=[pl.BlockSpec(memory_space=pltpu.VMEM)] * 5,
        out_specs=[pl.BlockSpec(memory_space=pltpu.VMEM)] * 3,
        scratch_shapes=[
            pltpu.VMEM((n, tokens, width), BF16),
            pltpu.VMEM((picks, tokens), F32),
            pltpu.VMEM((n, cap, tokens), BF16),
            pltpu.VMEM((n, cap, tokens), BF16),
            pltpu.VMEM((n, 1, cap), jnp.int32),
            pltpu.VMEM((n, table_rows, cap), BF16),
            pltpu.VMEM((table_rows, n * tokens), BF16),
            pltpu.VMEM((n, tokens, width), F32),
            pltpu.VMEM((n, tokens, width), BF16),
            pltpu.VMEM((n, tokens, width), BF16),
            pltpu.VMEM((n, tokens, cap), BF16),
            pltpu.VMEM((n, tokens, cap), BF16),
            pltpu.VMEM((pipes, picks, tokens), BF16),
            dma((2, n, CHUNKS)),
            dma((n, CHUNKS)),
            dma((n,)),
            dma((n,)),
            dma((n,)),
            dma((n,)),
            dma((2, n, CHUNKS)),
            dma((2, n, CHUNKS)),
            dma((n,)),
            dma((n,)),
            dma((pipes,)),
            dma((pipes,)),
        ],
        compiler_params=pltpu.CompilerParams(
            collective_id=0, has_side_effects=True, vmem_limit_bytes=40 * 1024 * 1024
        ),
    )(
        values,
        cotangent,
        scores.transpose(1, 2, 0),
        row_lists.reshape(n, 1, cap),
        sel_slot.transpose(1, 2, 0).reshape(picks, tokens),
    )
    return mem_out, grad_values, dscore.transpose(2, 0, 1)


def solution(mesh):
    body = shards_kernel if 2 <= mesh.shape["mem"] <= 4 else shards_collective
    placed = (
        P(("dp", "mem"), "pipe"),
        P(("dp", "mem"), "pipe"),
        P(("dp", "mem"), None, None),
        P(("dp", "mem"), None, None),
        P(("dp", "mem"), None, None),
    )
    return jax.shard_map(
        body,
        mesh=mesh,
        in_specs=placed,
        out_specs=(
            P(("dp", "mem"), "pipe"),
            P(("dp", "mem"), "pipe"),
            P(("dp", "mem"), None, None),
        ),
        check_vma=False,
    )
```

```python
import functools

import jax
import jax.numpy as jnp
from jax import lax
from jax.experimental import pallas as pl
from jax.experimental.pallas import tpu as pltpu
from jax.sharding import PartitionSpec as P


def shards_collective(values, cotangent, scores, row_lists, sel_slot):
    owners = lax.axis_size("mem")
    tokens_here = cotangent.shape[0]
    cap_slots = row_lists.shape[2]
    slot_count = owners * cap_slots
    width = values.shape[1]
    table_rows = values.shape[0]
    highest = lax.Precision.HIGHEST
    weights = jax.nn.softmax(scores, axis=-1)
    chosen = sel_slot.reshape(tokens_here, -1)
    owner_of = chosen // cap_slots
    place_of = chosen % cap_slots
    owner_hot = (owner_of[..., None] == jnp.arange(owners, dtype=jnp.int32)[None, None, :]).astype(
        jnp.float32
    )
    place_hot = (
        place_of[..., None] == jnp.arange(cap_slots, dtype=jnp.int32)[None, None, :]
    ).astype(jnp.float32)
    weighted_owner = owner_hot * weights.reshape(tokens_here, -1)[..., None]
    combined = jnp.einsum(
        "tpo,tpc->toc",
        weighted_owner,
        place_hot,
        precision=highest,
        preferred_element_type=jnp.float32,
    )
    combined = combined.reshape(tokens_here, slot_count).astype(jnp.bfloat16)
    asked = lax.all_to_all(row_lists[0], "mem", split_axis=0, concat_axis=0, tiled=True)
    present = asked >= 0
    looked = jnp.take(values, jnp.maximum(asked, 0), axis=0)
    looked = jnp.where(present[..., None], looked, jnp.zeros_like(looked))
    replied = lax.all_to_all(looked, "mem", split_axis=0, concat_axis=0, tiled=True)
    gathered_rows = replied.reshape(slot_count, width)
    mem_out = jnp.dot(combined, gathered_rows, preferred_element_type=jnp.float32).astype(
        jnp.bfloat16
    )
    products = lax.dot_general(
        cotangent, gathered_rows, (((1,), (1,)), ((), ())), preferred_element_type=jnp.float32
    )
    products = products.reshape(tokens_here, owners, cap_slots)
    picked = jnp.einsum(
        "tpc,toc->tpo", place_hot, products, precision=highest, preferred_element_type=jnp.float32
    )
    partial_dots = jnp.sum(picked * owner_hot, axis=-1).reshape(weights.shape)
    full_dots = lax.psum(partial_dots.astype(jnp.bfloat16), "pipe").astype(jnp.float32)
    grad_scores = weights * (full_dots - jnp.sum(weights * full_dots, axis=-1, keepdims=True))
    sums_here = lax.dot_general(
        combined, cotangent, (((0,), (0,)), ((), ())), preferred_element_type=jnp.float32
    )
    received = lax.all_to_all(
        sums_here.reshape(owners, cap_slots, width).astype(jnp.bfloat16),
        "mem",
        split_axis=0,
        concat_axis=0,
        tiled=True,
    ).astype(jnp.float32)
    received = received.reshape(-1, width)
    upper_part = received.astype(jnp.bfloat16)
    lower_part = (received - upper_part.astype(jnp.float32)).astype(jnp.bfloat16)
    row_hot = (
        asked.reshape(-1)[:, None] == jnp.arange(table_rows, dtype=jnp.int32)[None, :]
    ).astype(jnp.bfloat16)
    contract = (((0,), (0,)), ((), ()))
    grad_full = lax.dot_general(row_hot, upper_part, contract, preferred_element_type=jnp.float32)
    grad_full = grad_full + lax.dot_general(
        row_hot, lower_part, contract, preferred_element_type=jnp.float32
    )
    grad_values = grad_full.astype(jnp.bfloat16)
    return (mem_out, grad_values, grad_scores)


MESH = pl.DeviceIdType.MESH
CHUNKS = 2
F32 = jnp.float32
BF16 = jnp.bfloat16


def kernel(
    n,
    pipes,
    heads,
    topk,
    values_hbm,
    cot_ref,
    scores_hbm,
    rows_ref,
    sel_hbm,
    mem_ref,
    grad_ref,
    dscore_ref,
    values_ref,
    scores_ref,
    sel_ref,
    cot_all,
    weights,
    comb_own,
    comb_in,
    rows_in,
    hot,
    spread,
    part,
    from_left,
    from_right,
    prod_out,
    prod_in,
    dots_in,
    ag_send,
    ag_recv,
    cb_send,
    cb_recv,
    rl_send,
    rl_recv,
    rs_send,
    rs_recv,
    pr_send,
    pr_recv,
    dt_send,
    dt_recv,
    local_sem,
):
    me = lax.axis_index("mem")
    my_pipe = lax.axis_index("pipe")
    tokens, width = cot_ref.shape
    table_rows = values_hbm.shape[0]
    cap = rows_ref.shape[2]
    step = tokens // CHUNKS
    picks = heads * topk

    def peer(d):
        return lax.rem(me + d, n)

    def pipe_peer(d):
        return lax.rem(my_pipe + d, pipes)

    local = [
        pltpu.make_async_copy(src, dst, local_sem.at[i])
        for i, (src, dst) in enumerate(
            (
                (scores_hbm, scores_ref),
                (sel_hbm, sel_ref),
                (rows_ref.at[me], rows_in.at[me]),
                (cot_ref, cot_all.at[me]),
                (values_hbm, values_ref),
            )
        )
    ]
    for copy in local:
        copy.start()

    barrier = pltpu.get_barrier_semaphore()
    for d in range(1, n):
        pl.semaphore_signal(barrier, inc=1, device_id={"mem": peer(d)}, device_id_type=MESH)
    for d in range(1, pipes):
        pl.semaphore_signal(
            barrier, inc=1, device_id={"pipe": pipe_peer(d)}, device_id_type=MESH
        )
    pl.semaphore_wait(barrier, n - 1 + pipes - 1)

    def rows_of(c):
        return pl.ds(c * step, step)

    def gather_copy(side, source, c, own=False):
        to = me + 1 if side == 0 else me - 1
        src = cot_ref.at[rows_of(c)] if own else cot_all.at[source, rows_of(c)]
        return pltpu.make_async_remote_copy(
            src_ref=src,
            dst_ref=cot_all.at[source, rows_of(c)],
            send_sem=ag_send.at[side, source, c],
            recv_sem=ag_recv.at[source, c],
            device_id={"mem": to},
            device_id_type=MESH,
        )

    def sum_copy(side, dest, c):
        to = me + 1 if side == 0 else me - 1
        buf = from_left if side == 0 else from_right
        return pltpu.make_async_remote_copy(
            src_ref=buf.at[dest, rows_of(c)],
            dst_ref=buf.at[dest, rows_of(c)],
            send_sem=rs_send.at[side, dest, c],
            recv_sem=rs_recv.at[side, dest, c],
            device_id={"mem": to},
            device_id_type=MESH,
        )

    def list_copy(to):
        return pltpu.make_async_remote_copy(
            src_ref=rows_ref.at[to],
            dst_ref=rows_in.at[me],
            send_sem=rl_send.at[to],
            recv_sem=rl_recv.at[me],
            device_id={"mem": to},
            device_id_type=MESH,
        )

    def list_arrival(source):
        return pltpu.make_async_remote_copy(
            src_ref=rows_in.at[source],
            dst_ref=rows_in.at[source],
            send_sem=rl_send.at[source],
            recv_sem=rl_recv.at[source],
            device_id={"mem": source},
            device_id_type=MESH,
        )

    def comb_copy(to):
        return pltpu.make_async_remote_copy(
            src_ref=comb_own.at[to],
            dst_ref=comb_in.at[me],
            send_sem=cb_send.at[to],
            recv_sem=cb_recv.at[me],
            device_id={"mem": to},
            device_id_type=MESH,
        )

    def comb_arrival(source):
        return pltpu.make_async_remote_copy(
            src_ref=comb_in.at[source],
            dst_ref=comb_in.at[source],
            send_sem=cb_send.at[source],
            recv_sem=cb_recv.at[source],
            device_id={"mem": source},
            device_id_type=MESH,
        )

    def prod_copy(to):
        return pltpu.make_async_remote_copy(
            src_ref=prod_out.at[to],
            dst_ref=prod_in.at[me],
            send_sem=pr_send.at[to],
            recv_sem=pr_recv.at[me],
            device_id={"mem": to},
            device_id_type=MESH,
        )

    def prod_arrival(source):
        return pltpu.make_async_remote_copy(
            src_ref=prod_in.at[source],
            dst_ref=prod_in.at[source],
            send_sem=pr_send.at[source],
            recv_sem=pr_recv.at[source],
            device_id={"mem": source},
            device_id_type=MESH,
        )

    def dots_copy(to):
        return pltpu.make_async_remote_copy(
            src_ref=dots_in.at[my_pipe],
            dst_ref=dots_in.at[my_pipe],
            send_sem=dt_send.at[to],
            recv_sem=dt_recv.at[my_pipe],
            device_id={"pipe": to},
            device_id_type=MESH,
        )

    def dots_arrival(source):
        return pltpu.make_async_remote_copy(
            src_ref=dots_in.at[source],
            dst_ref=dots_in.at[source],
            send_sem=dt_send.at[source],
            recv_sem=dt_recv.at[source],
            device_id={"pipe": source},
            device_id_type=MESH,
        )

    for d in range(1, n):
        list_copy(peer(d)).start()
    for c in range(CHUNKS):

        @pl.when(me < n - 1)
        def _():
            gather_copy(0, me, c, own=True).start()

        @pl.when(me > 0)
        def _():
            gather_copy(1, me, c, own=True).start()

    local[0].wait()
    local[1].wait()
    scores = scores_ref[...]
    raised = jnp.exp(scores - jnp.max(scores, axis=1, keepdims=True))
    share = raised / jnp.sum(raised, axis=1, keepdims=True)
    weights[...] = share.reshape(picks, tokens)

    place = lax.broadcasted_iota(jnp.int32, (cap, tokens), 0)

    @pl.loop(0, n)
    def _(owner):
        first = owner * cap
        total = jnp.zeros((cap, tokens), F32)
        for h in range(heads):
            held = jnp.zeros((cap, tokens), F32)
            for k in range(topk):
                p = h * topk + k
                here = sel_ref[p : p + 1, :] - first
                held = jnp.where(place == here, weights[p : p + 1, :], held)
            total = total + held
        comb_own[owner] = total.astype(BF16)

    for d in range(1, n):
        comb_copy(peer(d)).start()
    comb_in[me] = comb_own[me]

    def relay(d):
        for c in range(CHUNKS):

            @pl.when(me - d >= 0)
            def _():
                gather_copy(0, me - d, c).wait_recv()

            @pl.when((me - d >= 0) & (me < n - 1))
            def _():
                gather_copy(0, me - d, c).start()

            @pl.when(me + d < n)
            def _():
                gather_copy(1, me + d, c).wait_recv()

            @pl.when((me + d < n) & (me > 0))
            def _():
                gather_copy(1, me + d, c).start()

    relay(1)
    for copy in local[2:]:
        copy.wait()

    row_ids = lax.broadcasted_iota(jnp.int32, (table_rows, cap), 0)
    for d in range(1, n):
        list_arrival(peer(d)).wait_recv()
        comb_arrival(peer(d)).wait_recv()
    for s in range(n):
        hot[s] = jnp.where(rows_in[s] == row_ids, 1.0, 0.0).astype(BF16)
        spread[:, s * tokens : (s + 1) * tokens] = jnp.dot(
            hot[s], comb_in[s], preferred_element_type=F32
        ).astype(BF16)
    part[...] = lax.dot_general(
        spread[...], values_ref[...], (((0,), (0,)), ((), ())), preferred_element_type=F32
    ).reshape(n, tokens, width)

    def open_line():
        for i in range(n - 1):

            @pl.when(me == 0)
            def _():
                from_left[n - 1 - i] = part[n - 1 - i].astype(BF16)
                for c in range(CHUNKS):
                    sum_copy(0, n - 1 - i, c).start()

            @pl.when(me == n - 1)
            def _():
                from_right[i] = part[i].astype(BF16)
                for c in range(CHUNKS):
                    sum_copy(1, i, c).start()

    def pass_on(t):
        right_dest = n - 1 - t + me
        left_dest = t - (n - 1 - me)
        for c in range(CHUNKS):
            at = rows_of(c)

            @pl.when((t >= me) & (me > 0))
            def _():
                sum_copy(0, right_dest, c).wait_recv()
                got = from_left[right_dest, at].astype(F32)
                from_left[right_dest, at] = (got + part[right_dest, at]).astype(BF16)
                sum_copy(0, right_dest, c).start()

            @pl.when((left_dest >= 0) & (me < n - 1))
            def _():
                sum_copy(1, left_dest, c).wait_recv()
                got = from_right[left_dest, at].astype(F32)
                from_right[left_dest, at] = (got + part[left_dest, at]).astype(BF16)
                sum_copy(1, left_dest, c).start()

    def products(source):
        full = lax.dot_general(
            cot_all[source],
            values_ref[...],
            (((1,), (1,)), ((), ())),
            preferred_element_type=F32,
        ).astype(BF16)
        prod_out[source] = jnp.dot(full, hot[source], preferred_element_type=F32).astype(BF16)

    def products_at(d):
        @pl.when(me - d >= 0)
        def _():
            products(me - d)
            prod_copy(me - d).start()

        @pl.when(me + d < n)
        def _():
            products(me + d)
            prod_copy(me + d).start()

    open_line()
    products(me)
    prod_in[me] = prod_out[me]
    products_at(1)
    for d in range(2, n):
        relay(d)
        pass_on(d - 1)
        products_at(d)

    for column in range(0, width, 256):
        grad_ref[:, column : column + 256] = jnp.dot(
            spread[...],
            cot_all[:, :, column : column + 256].reshape(n * tokens, 256),
            preferred_element_type=F32,
        ).astype(BF16)

    for d in range(1, n):
        prod_arrival(peer(d)).wait_recv()
    chosen = sel_ref[...].T
    place_of = lax.rem(chosen, cap)
    owner_of = lax.div(chosen, cap)
    dots = jnp.zeros((tokens, picks), F32)
    for o in range(n):
        found = jnp.take_along_axis(
            prod_in[o].astype(F32), place_of, axis=1, mode="promise_in_bounds"
        )
        dots = jnp.where(owner_of == o, found, dots)
    dots_in[my_pipe] = dots.T.astype(BF16)
    for d in range(1, pipes):
        dots_copy(pipe_peer(d)).start()

    for c in range(CHUNKS):
        at = rows_of(c)

        @pl.when((me > 0) & (me < n - 1))
        def _():
            sum_copy(0, me, c).wait_recv()
            sum_copy(1, me, c).wait_recv()
            both = from_left[me, at].astype(F32) + from_right[me, at].astype(F32)
            mem_ref[at] = (part[me, at] + both).astype(BF16)

        @pl.when(me == 0)
        def _():
            sum_copy(1, me, c).wait_recv()
            mem_ref[at] = (part[me, at] + from_right[me, at].astype(F32)).astype(BF16)

        @pl.when(me == n - 1)
        def _():
            sum_copy(0, me, c).wait_recv()
            mem_ref[at] = (part[me, at] + from_left[me, at].astype(F32)).astype(BF16)

    for d in range(1, pipes):
        dots_arrival(pipe_peer(d)).wait_recv()
    full_dots = dots_in[0].astype(F32)
    for q in range(1, pipes):
        full_dots = full_dots + dots_in[q].astype(F32)
    full_dots = full_dots.reshape(heads, topk, tokens)
    w = weights[...].reshape(heads, topk, tokens)
    dscore_ref[...] = w * (full_dots - jnp.sum(w * full_dots, axis=1, keepdims=True))

    for d in range(1, n):
        list_copy(peer(d)).wait_send()
        comb_copy(peer(d)).wait_send()
        prod_copy(peer(d)).wait_send()
    for d in range(1, pipes):
        dots_copy(pipe_peer(d)).wait_send()
    for c in range(CHUNKS):
        for d in range(n - 1):

            @pl.when((me - d >= 0) & (me < n - 1))
            def _():
                gather_copy(0, me - d, c, own=d == 0).wait_send()

            @pl.when((me + d < n) & (me > 0))
            def _():
                gather_copy(1, me + d, c, own=d == 0).wait_send()

        for t in range(n - 1):
            right_dest = n - 1 - t + me
            left_dest = t - (n - 1 - me)

            @pl.when(t >= me)
            def _():
                sum_copy(0, right_dest, c).wait_send()

            @pl.when(left_dest >= 0)
            def _():
                sum_copy(1, left_dest, c).wait_send()


def finish(mem_ref, grad_ref, dscore_ref, mem_out, grad_out, dscore_out, sems):
    pairs = ((grad_ref, grad_out), (mem_ref, mem_out), (dscore_ref, dscore_out))
    copies = [pltpu.make_async_copy(a, b, sems.at[i]) for i, (a, b) in enumerate(pairs)]
    for copy in copies:
        copy.start()
    for copy in copies:
        copy.wait()


def shards_kernel(values, cotangent, scores, row_lists, sel_slot):
    n, pipes = lax.axis_size("mem"), lax.axis_size("pipe")
    tokens, width = cotangent.shape
    heads, topk = scores.shape[1:]
    table_rows, cap = values.shape[0], row_lists.shape[2]
    picks = heads * topk
    dma = pltpu.SemaphoreType.DMA
    shapes = (
        jax.ShapeDtypeStruct((tokens, width), BF16),
        jax.ShapeDtypeStruct((table_rows, width), BF16),
        jax.ShapeDtypeStruct((heads, topk, tokens), F32),
    )
    results = pl.pallas_call(
        functools.partial(kernel, n, pipes, heads, topk),
        out_shape=shapes,
        in_specs=[pl.BlockSpec(memory_space=pl.ANY)] * 5,
        out_specs=[pl.BlockSpec(memory_space=pltpu.VMEM)] * 3,
        scratch_shapes=[
            pltpu.VMEM((table_rows, width), BF16),
            pltpu.VMEM((heads, topk, tokens), F32),
            pltpu.VMEM((picks, tokens), jnp.int32),
            pltpu.VMEM((n, tokens, width), BF16),
            pltpu.VMEM((picks, tokens), F32),
            pltpu.VMEM((n, cap, tokens), BF16),
            pltpu.VMEM((n, cap, tokens), BF16),
            pltpu.VMEM((n, 1, cap), jnp.int32),
            pltpu.VMEM((n, table_rows, cap), BF16),
            pltpu.VMEM((table_rows, n * tokens), BF16),
            pltpu.VMEM((n, tokens, width), F32),
            pltpu.VMEM((n, tokens, width), BF16),
            pltpu.VMEM((n, tokens, width), BF16),
            pltpu.VMEM((n, tokens, cap), BF16),
            pltpu.VMEM((n, tokens, cap), BF16),
            pltpu.VMEM((pipes, picks, tokens), BF16),
            dma((2, n, CHUNKS)),
            dma((n, CHUNKS)),
            dma((n,)),
            dma((n,)),
            dma((n,)),
            dma((n,)),
            dma((2, n, CHUNKS)),
            dma((2, n, CHUNKS)),
            dma((n,)),
            dma((n,)),
            dma((pipes,)),
            dma((pipes,)),
            dma((5,)),
        ],
        compiler_params=pltpu.CompilerParams(
            collective_id=0, has_side_effects=True, vmem_limit_bytes=63 * 1024 * 1024
        ),
    )(
        values,
        cotangent,
        scores.transpose(1, 2, 0),
        row_lists.reshape(n, 1, cap),
        sel_slot.transpose(1, 2, 0).reshape(picks, tokens),
    )
    mem_out, grad_values, dscore = pl.pallas_call(
        finish,
        out_shape=shapes,
        in_specs=[pl.BlockSpec(memory_space=pltpu.VMEM)] * 3,
        out_specs=[pl.BlockSpec(memory_space=pl.ANY)] * 3,
        scratch_shapes=[dma((3,))],
    )(*results)
    return mem_out, grad_values, dscore.transpose(2, 0, 1)


def solution(mesh):
    body = shards_kernel if 2 <= mesh.shape["mem"] <= 4 else shards_collective
    placed = (
        P(("dp", "mem"), "pipe"),
        P(("dp", "mem"), "pipe"),
        P(("dp", "mem"), None, None),
        P(("dp", "mem"), None, None),
        P(("dp", "mem"), None, None),
    )
    return jax.shard_map(
        body,
        mesh=mesh,
        in_specs=placed,
        out_specs=(
            P(("dp", "mem"), "pipe"),
            P(("dp", "mem"), "pipe"),
            P(("dp", "mem"), None, None),
        ),
        check_vma=False,
    )
```
